128 devices in a mesh: sub: 16 (over x, y), ifc: 8 (over z, core).
Axes of the slice: x: 4, y: 4, z: 4, core: 2. Of those that a mesh axis runs over, the one named last changes fastest.
Arguments:
- schur: bfloat16 [512, 1536, 1536], P(('sub', 'ifc')), as said below
- lam_start: bfloat16 [6144, 64, 128], P(('sub', 'ifc')), may hold values from -6 to 6
- rhs: float32 [6144, 64, 128], P(('sub', 'ifc')), may hold values from -24 to 24
- stiff: float32 [6144, 64], P(('sub', 'ifc')), may hold values from 1 to 6
- owner: int32 [512, 24, 1], replicated, may hold values from 0 to 127; in each aligned block of 96 rows (0 to 95, 96 to 191, ..., all dimensions but the last counted through in order) at most 2 rows name the same one
- local: int32 [512, 24], replicated, may hold values from 0 to 47
Outputs:
- lam_final: float32 [6144, 64, 128], P(('sub', 'ifc'))
- sens: float32 [512, 128], P(('sub', 'ifc'))
The draws below stay inside these ranges and needn't reach their ends.
Inputs may be any that keep to these rules, and one draw needn't show every extreme that they name: In the rows of one device (4 substructures of 24 slots) no owner is named more than 2 times, a bound that some block reaches. `schur`: each matrix is symmetric.
All inputs are finite; a program needn't handle non-finite values.
Results may differ from the reference program's by a relative error of at most 0.0008.
Values may be sent and summed in bfloat16 or wider, within the bound.
A program may use at most 128 MiB of HBM per device.

```python
import math
import jax
import jax.numpy as jnp
import numpy as np
from jax import lax

TILE = 64
NT = 24
ORDER = 1536
SUB_DEV = 4
R = 128
ITERS = 3
IF_DEV = 48
SUBS = 512
NIF = 6144
MOST = 2
DEVICES = 128


def draw_schur(key, part):
    key = jax.random.fold_in(key, 11)

    def single(index):
        inner = jax.random.fold_in(key, index)
        first, second = jax.random.split(inner)
        noise = jax.random.normal(first, (ORDER, ORDER), jnp.float32)
        center = jax.random.uniform(second, (ORDER,), jnp.float32, 5.0, 8.0)
        coupled = 2.0 * (noise + noise.T) / jnp.sqrt(2.0 * ORDER)
        return (jnp.diag(center) + coupled).astype(jnp.bfloat16)
    return lax.map(single, jnp.arange(SUBS))


def set_ends(entries, key, low, top_value):
    extent = entries.shape
    place = [jax.random.randint(jax.random.fold_in(key, axis), (), 0, extent[axis]) for axis in range(len(extent))]
    entries = entries.at[tuple(place)].set(low)
    longest = extent.index(max(extent))
    place[longest] = (place[longest] + 1) % extent[longest]
    return entries.at[tuple(place)].set(top_value)


def shard_levels(stream_key, shape, shards, smallest, top_value):
    loudness, own = 1.0, jax.random.fold_in(stream_key, 6)
    for dim, parts in shards:
        steps = jnp.exp(jax.random.uniform(jax.random.fold_in(own, dim), (parts,), jnp.float32, smallest / len(shards), top_value / len(shards)))
        loudness = loudness * jnp.repeat(steps, shape[dim] // parts).reshape([-1 if axis == dim else 1 for axis in range(len(shape))])
    return loudness


def routed_block(rng, own, number, rows, count, top, most, lean):
    ranking = jax.random.permutation(rng, count)
    heavy_load, usual = load_shares(count, rows * top, most, lean, True), load_shares(count, rows * top, most, lean, False)
    places = jnp.arange(count)

    def named(lengths, offset_by):
        used = int((lengths > 0).sum())
        fixed = max(1, used // 4)
        shifted = fixed + (places - fixed + offset_by * (used - fixed)) % max(1, count - fixed)
        return jnp.zeros((count,), jnp.int32).at[ranking[jnp.where(places < fixed, places, shifted)]].set(jnp.asarray(lengths, jnp.int32))

    lengths = jnp.where(number % 4 == 0, named(heavy_load, number // 4), named(usual, number - number // 4 - 1))
    mixed = jax.random.permutation(jax.random.fold_in(own, 3), count)
    giver, receiver = mixed[0:count // 2 * 2:2], mixed[1:count // 2 * 2:2]
    margin = jnp.minimum(lengths[giver] - 1, most - lengths[receiver]) // 2
    margin = jnp.where((giver == ranking[0]) | (receiver == ranking[0]) | (lengths[receiver] == 0), 0, jnp.maximum(margin, 0))
    shifted = jax.random.randint(jax.random.fold_in(own, 4), (count // 2,), 0, 1 << 20) % (margin + 1)
    lengths = lengths.at[giver].add(-shifted).at[receiver].add(shifted)
    items = jnp.searchsorted(jnp.cumsum(lengths), jnp.arange(rows * top), side="right").astype(jnp.int32)
    table = items.reshape(top, rows).T
    table = table[jax.random.permutation(jax.random.fold_in(own, 1), rows)]
    offset_by = jax.random.randint(jax.random.fold_in(own, 2), (rows, 1), 0, top)
    return jnp.take_along_axis(table, (jnp.arange(top)[None, :] + offset_by) % top, axis=1)


def load_shares(amount, total, limit, skew, full):
    portions = [(1 << 20) // math.isqrt(grade ** skew) + 1 for grade in range(1, amount + 1)]
    largest = limit if full else min(limit, max(-(-total // amount), total * portions[0] // sum(portions)))
    least = 1 if total - largest >= amount - 1 else 0
    counts, rest = [largest] + [least] * (amount - 1), total - largest - least * (amount - 1)
    while rest > 0:
        candidates = [i for i in range(1, amount) if counts[i] < largest] or [i for i in range(1, amount) if counts[i] < limit]
        pool, budget = sum([portions[i] for i in candidates]), rest
        for i in candidates:
            more = min(limit - counts[i], max(1, budget * portions[i] // pool), rest)
            counts[i] = counts[i] + more
            rest = rest - more
    return np.array(counts)


def gaussian(rng, extent, width, reach, cuts=(), kind=jnp.bfloat16):
    array = jax.random.normal(rng, extent, jnp.float32) * width
    if len(cuts) > 0:
        array = shard_levels(rng, extent, cuts, -0.22, 0.18) * array
    return jnp.clip(array, min=-reach, max=reach).astype(kind)


def setup_inputs(seed: int = 0) -> dict:
    keys = jax.random.split(jax.random.key(seed), 7)
    schur = draw_schur(jax.random.fold_in(keys[6], 71), 0)
    lam_start = gaussian(keys[1], (NIF, TILE, R), 1.0, 6.0, ((0, 128),))
    rhs = gaussian(keys[2], (NIF, TILE, R), 4.0, 24.0, ((0, 128),), jnp.float32)
    stiff = jnp.clip(1.0 + 5.0 * jax.random.uniform(keys[3], (NIF, TILE), jnp.float32) ** shard_levels(keys[3], (NIF, TILE), ((0, 128),), -0.2, 0.2), 1.0, 6.0)
    owner_keys = jax.random.split(jax.random.fold_in(keys[4], 1), SUBS * NT // (SUB_DEV * NT))
    owner_turns = jax.random.permutation(jax.random.fold_in(keys[4], 3), SUBS * NT // (SUB_DEV * NT))
    owner = jax.vmap(lambda own, number: routed_block(jax.random.fold_in(keys[4], 2), own, number, SUB_DEV * NT, DEVICES, 1, MOST, 2))(owner_keys, owner_turns).reshape((SUBS, NT, 1))
    local = set_ends(jax.random.randint(keys[5], (SUBS, NT), 0, IF_DEV), jax.random.fold_in(keys[5], 1), 0, IF_DEV - 1).astype(jnp.int32)
    return dict(schur=schur, lam_start=lam_start, rhs=rhs, stiff=stiff, owner=owner, local=local)


OMEGA = 0.7


def reference(schur, lam_start, rhs, stiff, owner, local):
    gid = (owner[:, :, 0] * IF_DEV + local).reshape(-1).astype(jnp.int32)
    diag_vals = jnp.diagonal(schur, axis1=1, axis2=2).astype(jnp.float32)
    dsum = jnp.zeros((NIF, TILE), jnp.float32).at[gid].add(diag_vals.reshape(SUBS * NT, TILE))
    dtotal = stiff + dsum
    lam = lam_start.astype(jnp.float32)

    def apply_one(pair):
        return jnp.dot(pair[0], pair[1], preferred_element_type=jnp.float32)

    gathered = None
    image = None
    for sweep in range(ITERS):
        lamb = lam.astype(jnp.bfloat16)
        gathered = lamb[gid].reshape(SUBS, ORDER, R)
        image = lax.map(apply_one, (schur, gathered))
        rounded = image.astype(jnp.bfloat16).astype(jnp.float32).reshape(SUBS * NT, TILE, R)
        assembled = jnp.zeros((NIF, TILE, R), jnp.float32).at[gid].add(rounded)
        resid = rhs - stiff[:, :, None] * lam - assembled
        lam = lam + OMEGA * resid / dtotal[:, :, None]
    sens = -jnp.sum(gathered.astype(jnp.float32) * image, axis=1) / ORDER
    return lam, sens
```

```python
import functools

import jax
import jax.numpy as jnp
from jax import lax
from jax.experimental import pallas as pl
from jax.experimental.pallas import tpu as pltpu
from jax.sharding import PartitionSpec as P

ITERS = 3
OMEGA = 0.7
MESH = pl.DeviceIdType.MESH
NP = 4
LANES = 128
CAPS = (11, 16)


def kernel(
    cap, tab, s_hbm, lam0, rhs, stiff_t, slot_tile,
    lam, sens,
    s_buf, z, ybf, w, st, run, psum, packed, rc, r1, r2, drow, dsend, drecv, dpart, drc, dx, dfull,
    *rest,
):
    pool, arecv, rrecv = rest[0:NP], rest[NP : 2 * NP], rest[2 * NP : 3 * NP]
    (sem_s, sem_l, g1s, g1r, g2s, g2r, gcs, gcr, as_, ar, bs, br, rcs, rcr, r1s, r1r, r2s, r2r, ds, dr) = rest[3 * NP :]
    nsub, order, _ = s_buf.shape
    nif, tile, width = lam.shape
    rp = tile // NP
    slots = 16 * cap
    half = nif // 2
    line = 4 * nif
    a, b = lax.axis_index("sub"), lax.axis_index("ifc")
    x, y, zz, c = a // 4, a % 4, b // 2, b % 2
    xp, xm, x2 = (x + 1) % 4, (x + 3) % 4, (x + 2) % 4
    j_me = y * 4 + zz
    to_p, to_m, to_2 = (xp * 4 + y, b), (xm * 4 + y, b), (x2 * 4 + y, b)
    to_c = (a, zz * 2 + 1 - c)
    o_t1, o_t2, o_t3 = 0, slots, slots + 96
    o_ord, o_last = 2 * slots + 96, 3 * slots + 96

    def plane(i):
        py, pz = (y + i // 4) % 4, (zz + i % 4) % 4
        return py * 4 + pz, (x * 4 + py, pz * 2 + c)

    def remote(src, dst, ssem, rsem, dev):
        return pltpu.make_async_remote_copy(
            src_ref=src, dst_ref=dst, send_sem=ssem, recv_sem=rsem, device_id=dev, device_id_type=MESH
        )

    def wait_on(ref, sem):
        pltpu.make_async_copy(ref, ref, sem).wait()

    load_s = pltpu.make_async_copy(s_hbm, s_buf, sem_s)
    load_s.start()

    barrier = pltpu.get_barrier_semaphore()
    for dev in (to_p, to_m, to_2, to_c):
        pl.semaphore_signal(barrier, inc=1, device_id=dev, device_id_type=MESH)

    @pl.loop(1, 16)
    def _(i):
        pl.semaphore_signal(barrier, inc=1, device_id=plane(i)[1], device_id_type=MESH)

    @pl.loop(0, nif)
    def _(l):
        lam[l] = lam0[l].astype(jnp.float32)

    pl.semaphore_wait(barrier, 19)

    def at(core, xx, lo=0, n=nif):
        return pl.ds((core * 4 + xx) * nif + lo, n)

    def g0(p):
        rows = slice(p * rp, (p + 1) * rp)
        base = (c * 4 + x) * nif

        @pl.loop(0, nif // 8)
        def _(l):
            pool[p][pl.ds(base + l * 8, 8)] = lam[pl.ds(l * 8, 8), rows].astype(jnp.bfloat16)

        own = pool[p].at[at(c, x)]
        remote(own, own, g1s.at[p, 0], g1r.at[p, 0], to_p).start()
        remote(own, own, g1s.at[p, 1], g1r.at[p, 1], to_m).start()

    def g1(p):
        wait_on(pool[p].at[at(c, xm)], g1r.at[p, 0])
        one = pool[p].at[at(c, xm, 0, half)]
        remote(one, one, g2s.at[p, 0], g2r.at[p, 0], to_p).start()
        wait_on(pool[p].at[at(c, xp)], g1r.at[p, 1])
        two = pool[p].at[at(c, xp, half, half)]
        remote(two, two, g2s.at[p, 1], g2r.at[p, 1], to_m).start()

    def g2(p):
        wait_on(pool[p].at[at(c, x2, 0, half)], g2r.at[p, 0])
        wait_on(pool[p].at[at(c, x2, half, half)], g2r.at[p, 1])
        mine = pool[p].at[pl.ds(c * line, line)]
        remote(mine, mine, gcs.at[p], gcr.at[p], to_c).start()

    def g3(p):
        wait_on(pool[p].at[pl.ds((1 - c) * line, line)], gcr.at[p])

        @pl.loop(0, 16)
        def _(j):
            for k in range(cap):
                q = j * cap + k
                packed[p, q] = pool[p][tab[o_t1 + q]]

        @pl.loop(1, 16)
        def _(i):
            j, dev = plane(i)
            remote(
                packed.at[p, pl.ds(j * cap, cap)], arecv[p].at[pl.ds(j_me * cap, cap)], as_.at[p], ar.at[p], dev
            ).start()

        own = pl.ds(j_me * cap, cap)
        copy = pltpu.make_async_copy(packed.at[p, own], arecv[p].at[own], sem_l)
        copy.start()
        copy.wait()

    def a1(p):
        wait_on(arecv[p].at[pl.ds(0, 15 * cap)], ar.at[p])

        @pl.loop(0, 96 // 8)
        def _(i):
            for u in range(8):
                t = i * 8 + u
                z[t, p * rp : (p + 1) * rp] = arecv[p][tab[o_t2 + t]]

    def multiply(last):
        zz_ = z.reshape(nsub, order, width)
        yy_ = ybf.reshape(nsub, order, width)
        chunk = 256

        @pl.loop(0, nsub)
        def _(s):
            def part(m, acc):
                rows = pl.ds(m * chunk, chunk)
                out = jnp.dot(s_buf[s, rows, :], zz_[s], preferred_element_type=jnp.float32)
                yy_[s, rows, :] = out.astype(jnp.bfloat16)
                prod = out * zz_[s, rows, :].astype(jnp.float32)
                return acc + jnp.sum(prod.reshape(chunk // 8, 8, width), axis=0)

            acc = lax.fori_loop(0, order // chunk, part, jnp.zeros((8, width), jnp.float32))

            @pl.when(last)
            def _():
                sens[s] = -jnp.sum(acc, axis=0, keepdims=True) / order

    def r0(p):
        wait_on(pool[p].at[at(c, x)], g1s.at[p, 0])
        wait_on(pool[p].at[at(c, x)], g1s.at[p, 1])
        wait_on(pool[p].at[at(c, xm, 0, half)], g2s.at[p, 0])
        wait_on(pool[p].at[at(c, xp, half, half)], g2s.at[p, 1])
        wait_on(pool[p].at[pl.ds(c * line, line)], gcs.at[p])
        wait_on(packed.at[p, pl.ds(0, 15 * cap)], as_.at[p])

        @pl.loop(0, 16)
        def _(j):
            for k in range(cap):
                q = j * cap + k
                packed[p, q] = ybf[tab[o_t3 + q], p * rp : (p + 1) * rp]

        @pl.loop(1, 16)
        def _(i):
            j, dev = plane(i)
            remote(
                packed.at[p, pl.ds(j * cap, cap)], rrecv[p].at[pl.ds(j_me * cap, cap)], bs.at[p], br.at[p], dev
            ).start()

        own = pl.ds(j_me * cap, cap)
        copy = pltpu.make_async_copy(packed.at[p, own], rrecv[p].at[own], sem_l)
        copy.start()
        copy.wait()

    def ra(p):
        wait_on(rrecv[p].at[pl.ds(0, 15 * cap)], br.at[p])
        wait_on(packed.at[p, pl.ds(0, 15 * cap)], bs.at[p])

        def add(q8, acc):
            for u in range(8):
                q = q8 * 8 + u
                code = tab[o_ord + q]
                got = rrecv[p][code // 2].astype(jnp.float32)
                acc = jnp.where(code % 2 == 1, 0.0, acc) + got
                run[q] = acc
            return acc

        lax.fori_loop(0, slots // 8, add, jnp.zeros((rp, width), jnp.float32))

        @pl.loop(0, 2 * line // 8)
        def _(t8):
            for u in range(8):
                t = t8 * 8 + u
                pos = tab[o_last + t]
                total = run[jnp.maximum(pos, 0)]
                psum[p, t] = jnp.where(pos >= 0, total, 0.0).astype(jnp.bfloat16)

        remote(psum.at[p, pl.ds((1 - c) * line, line)], rc.at[p], rcs.at[p], rcr.at[p], to_c).start()

    def add_to(p, start, other, n):
        @pl.loop(0, n // 8)
        def _(i):
            here = pl.ds(start + i * 8, 8)
            total = psum[p, here].astype(jnp.float32) + other[pl.ds(i * 8, 8)].astype(jnp.float32)
            psum[p, here] = total.astype(jnp.bfloat16)

    def rb(p):
        wait_on(rc.at[p], rcr.at[p])
        add_to(p, c * line, rc.at[p], line)
        remote(psum.at[p, at(c, x2, 0, half)], r1.at[p, 0], r1s.at[p, 0], r1r.at[p, 0], to_p).start()
        remote(psum.at[p, at(c, x2, half, half)], r1.at[p, 1], r1s.at[p, 1], r1r.at[p, 1], to_m).start()

    def rcc(p):
        wait_on(r1.at[p, 0], r1r.at[p, 0])
        add_to(p, (c * 4 + xp) * nif, r1.at[p, 0], half)
        remote(psum.at[p, at(c, xp)], r2.at[p, 0], r2s.at[p, 0], r2r.at[p, 0], to_p).start()
        wait_on(r1.at[p, 1], r1r.at[p, 1])
        add_to(p, (c * 4 + xm) * nif + half, r1.at[p, 1], half)
        remote(psum.at[p, at(c, xm)], r2.at[p, 1], r2s.at[p, 1], r2r.at[p, 1], to_m).start()

    def rd(p):
        rows = slice(p * rp, (p + 1) * rp)
        wait_on(r2.at[p, 0], r2r.at[p, 0])
        wait_on(r2.at[p, 1], r2r.at[p, 1])
        base = (c * 4 + x) * nif

        @pl.loop(0, nif // 4)
        def _(l4):
            ls = pl.ds(l4 * 4, 4)
            asm = (
                psum[p, pl.ds(base + l4 * 4, 4)].astype(jnp.float32)
                + r2[p, 0, ls].astype(jnp.float32)
                + r2[p, 1, ls].astype(jnp.float32)
            )
            old = lam[ls, rows]
            lam[ls, rows] = old + (rhs[ls, rows] - st[ls, rows] * old - asm) * w[ls, rows]

        wait_on(psum.at[p, pl.ds((1 - c) * line, line)], rcs.at[p])
        wait_on(r1.at[p, 0], r1s.at[p, 0])
        wait_on(r1.at[p, 1], r1s.at[p, 1])
        wait_on(r2.at[p, 0], r2s.at[p, 0])
        wait_on(r2.at[p, 1], r2s.at[p, 1])

    def diag():
        load_s.wait()
        lane = lax.broadcasted_iota(jnp.int32, (tile, LANES), 1)
        row = lax.broadcasted_iota(jnp.int32, (tile, LANES), 0)
        for k in range(order // tile):
            lo = k // 2 * LANES
            keep = lane == row + (k % 2) * tile

            @pl.loop(0, nsub)
            def _(s):
                blk = s_buf[s, k * tile : (k + 1) * tile, lo : lo + LANES].astype(jnp.float32)
                picked = jnp.sum(jnp.where(keep, blk, 0.0), axis=0, keepdims=True)
                if k % 2:
                    picked = pltpu.roll(picked, tile, 1)
                drow[s * (order // tile) + k] = picked

        @pl.loop(0, 16)
        def _(j):
            for k in range(cap):
                dsend[pl.ds(j * 16 + k, 1), :] = drow[tab[o_t3 + j * cap + k]]
            for k in range(cap, 16):
                dsend[pl.ds(j * 16 + k, 1), :] = jnp.zeros((1, LANES), jnp.float32)

        @pl.loop(1, 16)
        def _(i):
            j, dev = plane(i)
            remote(dsend.at[pl.ds(j * 16, 16)], drecv.at[pl.ds(j_me * 16, 16)], ds.at[0], dr.at[0], dev).start()

        own = pl.ds(j_me * 16, 16)
        copy = pltpu.make_async_copy(dsend.at[own], drecv.at[own], sem_l)
        copy.start()
        copy.wait()

    def diag2():
        wait_on(drecv.at[pl.ds(0, 240)], dr.at[0])
        wait_on(dsend.at[pl.ds(0, 240)], ds.at[0])
        came = drecv[...].astype(jnp.bfloat16)
        for h in range(2 * line // LANES):
            want = lax.broadcasted_iota(jnp.int32, (LANES, 256), 0) + h * LANES
            hot = jnp.where(want == slot_tile[...], 1.0, 0.0).astype(jnp.bfloat16)
            dpart[h * LANES : (h + 1) * LANES] = jnp.dot(hot, came, preferred_element_type=jnp.float32)
        remote(dpart.at[pl.ds((1 - c) * line, line)], drc, ds.at[1], dr.at[1], to_c).start()

    def diag3():
        wait_on(drc, dr.at[1])
        mine = pl.ds(c * line, line)
        dpart[mine] += drc[...]
        wait_on(drc, ds.at[1])
        for i, (xt, dev) in enumerate(((xp, to_p), (xm, to_m), (x2, to_2))):
            remote(dpart.at[at(c, xt)], dx.at[i], ds.at[2 + i], dr.at[2 + i], dev).start()

    def diag4():
        for i in range(3):
            wait_on(dx.at[i], dr.at[2 + i])
        dfull[...] = jnp.zeros_like(dfull)
        dfull[0:nif] = dpart[at(c, x)] + dx[0] + dx[1] + dx[2]
        for i in range(3):
            wait_on(dx.at[i], ds.at[2 + i])
        stt = stiff_t[...]
        inv = OMEGA / (stt + dfull[...].T[0:tile])
        for g in range(nif):
            w[g] = jnp.broadcast_to(inv[:, g : g + 1], (tile, width))
            st[g] = jnp.broadcast_to(stt[:, g : g + 1], (tile, width))

    for p in range(NP):
        g0(p)
    diag()
    diag2()
    diag3()
    diag4()

    @pl.loop(0, ITERS)
    def _(sweep):
        for t in range(NP + 3):
            for j, stage in reversed(list(enumerate((g1, g2, g3, a1)))):
                if 0 <= t - j < NP:
                    stage(t - j)
        multiply(sweep == ITERS - 1)
        for p in range(NP):
            r0(p)

        def rd_g0(p):
            rd(p)

            @pl.when(sweep < ITERS - 1)
            def _():
                g0(p)

        for t in range(NP + 3):
            for j, stage in reversed(list(enumerate((ra, rb, rcc, rd_g0)))):
                if 0 <= t - j < NP:
                    stage(t - j)


def sweeps(cap, cid, schur, lam_start, rhs, stiff, all_owner, all_local):
    nsub, order, _ = schur.shape
    nif, tile, width = lam_start.shape
    i32 = jnp.int32
    a, b = lax.axis_index("sub"), lax.axis_index("ifc")
    x, y, zz, c = a // 4, a % 4, b // 2, b % 2
    j_me = y * 4 + zz
    me = a * 8 + b
    slots = 16 * cap

    grid = (4, 4, 4, 2, 96)
    own5 = lax.dynamic_slice(all_owner.reshape(grid), (x, 0, 0, c, 0), (1, 4, 4, 1, 96)).reshape(16, 96)
    loc5 = lax.dynamic_slice(all_local.reshape(grid), (x, 0, 0, c, 0), (1, 4, 4, 1, 96)).reshape(16, 96)
    here = (own5 // 2) % 16 == j_me
    before = jnp.arange(96)[:, None] < jnp.arange(96)[None, :]
    rank = jnp.sum((here[:, :, None] & before[None]).astype(i32), axis=1)
    tid = ((own5 % 2) * 4 + own5 // 32) * nif + loc5
    match = here[:, :, None] & (rank[:, :, None] == jnp.arange(cap)[None, None, :])
    slot_tile = jnp.sum(jnp.where(match, tid[:, :, None] + 1, 0), axis=1) - 1
    flat = slot_tile.reshape(slots)
    t1 = jnp.maximum(flat, 0)
    seat = jnp.arange(slots)
    val = jnp.where(flat < 0, 8 * nif, flat)
    key = val * 256 + seat
    pos = jnp.sum((key[None, :] < key[:, None]).astype(i32), axis=1)
    first = ~jnp.any((val[None, :] == val[:, None]) & (seat[None, :] < seat[:, None]), axis=1)
    code = seat * 2 + first.astype(i32)
    order_tab = jnp.sum(jnp.where(pos[:, None] == seat[None, :], code[:, None], 0), axis=0)
    tiles = jnp.arange(8 * nif)
    upto = jnp.sum((val[None, :] <= tiles[:, None]).astype(i32), axis=1)
    has = jnp.any(val[None, :] == tiles[:, None], axis=1)
    last = jnp.where(has, upto - 1, -1)

    mine = lax.dynamic_slice_in_dim(all_owner, me, 1, 0)[0]
    group = (mine // 2) % 16
    same = (group[None, :] == group[:, None]) & (jnp.arange(96)[None, :] < jnp.arange(96)[:, None])
    t2 = group * cap + jnp.sum(same.astype(i32), axis=1)
    t3 = jnp.sum(jnp.where(t2[:, None] == seat[None, :], jnp.arange(96)[:, None], 0), axis=0)
    tab = jnp.concatenate([t1, t2, t3, order_tab, last]).astype(i32)
    wide = jnp.pad(slot_tile, ((0, 0), (0, 16 - cap)), constant_values=-1).reshape(1, 256)
    stiff_t = jnp.pad(stiff, ((0, LANES - nif), (0, 0)), constant_values=1.0).T

    rp = tile // NP
    bf, f32 = jnp.bfloat16, jnp.float32
    vm = pltpu.VMEM
    dma = pltpu.SemaphoreType.DMA
    line = 4 * nif
    scratch = [
        vm((nsub, order, order), bf),
        vm((96, tile, width), bf),
        vm((96, tile, width), bf),
        vm((nif, tile, width), f32),
        vm((nif, tile, width), f32),
        vm((slots, rp, width), f32),
        vm((NP, 2 * line, rp, width), bf),
        vm((NP, slots, rp, width), bf),
        vm((NP, line, rp, width), bf),
        vm((NP, 2, nif // 2, rp, width), bf),
        vm((NP, 2, nif, rp, width), bf),
        vm((96, 1, LANES), f32),
        vm((256, LANES), f32),
        vm((256, LANES), f32),
        vm((2 * line, LANES), f32),
        vm((line, LANES), f32),
        vm((3, nif, LANES), f32),
        vm((LANES, LANES), f32),
    ]
    scratch += [vm((2 * line, rp, width), bf)] * NP
    scratch += [vm((slots, rp, width), bf)] * (2 * NP)
    scratch += [dma, dma]
    scratch += [dma((NP, 2))] * 4 + [dma((NP,))] * 8 + [dma((NP, 2))] * 4 + [dma((5,))] * 2
    in_vm = pl.BlockSpec(memory_space=vm)
    lam, sens = pl.pallas_call(
        functools.partial(kernel, cap),
        out_shape=(
            jax.ShapeDtypeStruct((nif, tile, width), f32),
            jax.ShapeDtypeStruct((nsub, 1, width), f32),
        ),
        in_specs=[pl.BlockSpec(memory_space=pltpu.SMEM), pl.BlockSpec(memory_space=pl.ANY), in_vm, in_vm, in_vm, in_vm],
        out_specs=(in_vm, in_vm),
        scratch_shapes=scratch,
        compiler_params=pltpu.CompilerParams(
            collective_id=cid, has_side_effects=True, vmem_limit_bytes=63 * 2**20
        ),
        name=f"sweeps_{cap}",
    )(tab, schur, lam_start, rhs, stiff_t, wide)
    return lam, sens.reshape(nsub, width)


def body(schur, lam_start, rhs, stiff, owner, local):
    all_owner = owner.reshape(128, 96)
    all_local = local.reshape(128, 96)
    group = (all_owner // 2) % 16
    most = jnp.max(jnp.sum((group[:, :, None] == jnp.arange(16)).astype(jnp.int32), axis=1))
    args = (schur, lam_start, rhs, stiff, all_owner, all_local)
    return lax.cond(
        most <= CAPS[0],
        functools.partial(sweeps, CAPS[0], 0),
        functools.partial(sweeps, CAPS[1], 1),
        *args,
    )


def solution(mesh):
    spec = P(("sub", "ifc"), None, None)
    return jax.shard_map(
        body,
        mesh=mesh,
        in_specs=(spec, spec, spec, P(("sub", "ifc"), None), P(), P()),
        out_specs=(spec, P(("sub", "ifc"), None)),
        check_vma=False,
    )
```

```python
import functools

import jax
import jax.numpy as jnp
from jax import lax
from jax.experimental import pallas as pl
from jax.experimental.pallas import tpu as pltpu
from jax.sharding import PartitionSpec as P

ITERS = 3
OMEGA = 0.7
MESH = pl.DeviceIdType.MESH
NP = 4
LANES = 128
BLOCKS = 32
PLANS = ((0, 0, 5), (1, 0, 5), (2, 0, 5), (2, 0, 6), (0, 0, 8))


def pairing(kind, u):
    swap, mirror = u + 1 - 2 * (u % 2), 3 - u
    if kind == 0:
        return u // 2, u % 2, swap, mirror
    return ((u + 1) // 2) % 2, u // 2, mirror, swap


def split(axis, x, y, z):
    return ((x, y, z), (y, x, z), (z, x, y))[axis]


def join(axis, u, v, w):
    return ((u, v, w), (v, u, w), (v, w, u))[axis]


def kernel(
    axis, kind, cap, tab, s_hbm, lam0, rhs, stiff_t, slot_tile,
    lam, sens,
    s_buf, z, ybf, w_inv, st, run, psum, packed, rc, r1, half, drow, dsend, drecv, dpart, drc, dx, dfull,
    *rest,
):
    pool, arecv, rrecv = rest[0:NP], rest[NP : 2 * NP], rest[2 * NP : 3 * NP]
    sem_s, sem_l, g0s, g0r, g1s, g1r, as_, ar, bs, br, rcs, rcr, r1s, r1r, ds, dr = rest[3 * NP :]
    nsub, per_sub, _, rp, order = s_buf.shape
    nif, tile, width = lam.shape
    slots = BLOCKS * cap
    both = 2 * nif
    ntiles = nsub * per_sub
    a, b = lax.axis_index("sub"), lax.axis_index("ifc")
    c = b % 2
    u, v, w = split(axis, a // 4, a % 4, b // 2)
    _, place, mate, across = pairing(kind, u)

    def dev(uu, vv, ww, cc):
        x, y, zz = join(axis, uu, vv, ww)
        return (x * 4 + y, zz * 2 + cc)

    to_mate, to_core = dev(mate, v, w, c), dev(u, v, w, 1 - c)
    me_v, me_w = [(v + i) % 4 for i in range(4)], [(w + i) % 4 for i in range(4)]
    seat = [v * 4 + w, 16 + v * 4 + w]
    o_t1, o_t2, o_t3 = 0, slots, slots + ntiles
    o_ord, o_last = 2 * slots + ntiles, 3 * slots + ntiles

    def remote(src, dst, ssem, rsem, to):
        return pltpu.make_async_remote_copy(
            src_ref=src, dst_ref=dst, send_sem=ssem, recv_sem=rsem, device_id=to, device_id_type=MESH
        )

    def wait_on(ref, sem):
        pltpu.make_async_copy(ref, ref, sem).wait()

    def partners(visit):
        def row(vv, first):
            for i in range(first, 4):
                for side, uu in enumerate((u, across)):
                    visit(side, side * 16 + vv * 4 + me_w[i], dev(uu, vv, me_w[i], c))

        visit(1, seat[1], dev(across, v, w, c))
        row(v, 1)

        @pl.loop(1, 4)
        def _(i):
            row((v + i) % 4, 0)

    def scatter(src, dst, n, ssem, rsem):
        def send(side, block, to):
            remote(src.at[pl.ds(block * n, n)], dst.at[pl.ds(seat[side] * n, n)], ssem, rsem, to).start()

        partners(send)
        own = pl.ds(seat[0] * n, n)
        copy = pltpu.make_async_copy(src.at[own], dst.at[own], sem_l)
        copy.start()
        copy.wait()

    load_s = pltpu.make_async_copy(s_hbm, s_buf, sem_s)
    load_s.start()

    barrier = pltpu.get_barrier_semaphore()
    for to in (to_mate, to_core):
        pl.semaphore_signal(barrier, inc=1, device_id=to, device_id_type=MESH)
    partners(lambda side, block, to: pl.semaphore_signal(barrier, inc=1, device_id=to, device_id_type=MESH))

    @pl.loop(0, nif)
    def _(l):
        lam[l] = lam0[l].astype(jnp.float32)

    run[slots] = jnp.zeros((rp, width), jnp.float32)
    sens[...] = jnp.zeros_like(sens)
    pl.semaphore_wait(barrier, BLOCKS + 1)

    def at(core, which):
        return pl.ds((core * 2 + which) * nif, nif)

    def core_part(core):
        return pl.ds(core * both, both)

    def rows(p):
        return slice(p * rp, (p + 1) * rp)

    others = (BLOCKS - 1) * cap

    def g0(p):
        base = (c * 2 + place) * nif

        @pl.loop(0, nif // 8)
        def _(l):
            pool[p][pl.ds(base + l * 8, 8)] = lam[pl.ds(l * 8, 8), rows(p)].astype(jnp.bfloat16)

        own = pool[p].at[at(c, place)]
        remote(own, own, g0s.at[p], g0r.at[p], to_mate).start()

    def g1(p):
        wait_on(pool[p].at[at(c, 1 - place)], g0r.at[p])
        mine = pool[p].at[core_part(c)]
        remote(mine, mine, g1s.at[p], g1r.at[p], to_core).start()

    def g2(p):
        wait_on(pool[p].at[core_part(1 - c)], g1r.at[p])

        @pl.loop(0, slots // 16)
        def _(j):
            for k in range(16):
                q = j * 16 + k
                packed[p, q] = pool[p][tab[o_t1 + q]]

        if p > 1:
            wait_on(packed.at[p - 2, pl.ds(0, others)], as_.at[p - 2])
        scatter(packed.at[p], arecv[p], cap, as_.at[p], ar.at[p])

    def a1(p):
        wait_on(arecv[p].at[pl.ds(0, others)], ar.at[p])

        @pl.loop(0, ntiles // 16)
        def _(i):
            for k in range(16):
                t = i * 16 + k
                z[t, rows(p)] = arecv[p][tab[o_t2 + t]]

    def mm(p, last):
        flat = z.reshape(nsub, order, width)
        parts = z.reshape(nsub, per_sub, tile, width)
        outs = ybf.reshape(nsub, per_sub, tile, width)
        n = per_sub * rp

        @pl.loop(0, nsub)
        def _(s):
            lhs = s_buf[s, :, p].reshape(n, order)
            out = jnp.dot(lhs, flat[s], preferred_element_type=jnp.float32)
            outs[s, :, rows(p)] = out.astype(jnp.bfloat16).reshape(per_sub, rp, width)

            @pl.when(last)
            def _():
                prod = out * parts[s, :, rows(p)].reshape(n, width).astype(jnp.float32)
                sens[s] -= jnp.sum(prod, axis=0, keepdims=True) / order

    def r0(p):
        wait_on(pool[p].at[at(c, place)], g0s.at[p])
        wait_on(pool[p].at[core_part(c)], g1s.at[p])
        if p >= NP - 2:
            wait_on(packed.at[p, pl.ds(0, others)], as_.at[p])

        @pl.loop(0, slots // 16)
        def _(j):
            for k in range(16):
                q = j * 16 + k
                packed[p, q] = ybf[tab[o_t3 + q], rows(p)]

    def rs(p):
        if p > 1:
            wait_on(packed.at[p - 2, pl.ds(0, others)], bs.at[p - 2])
        scatter(packed.at[p], rrecv[p], cap, bs.at[p], br.at[p])

    def ra(p):
        wait_on(rrecv[p].at[pl.ds(0, others)], br.at[p])
        if p >= NP - 2:
            wait_on(packed.at[p, pl.ds(0, others)], bs.at[p])

        def add(q8, acc):
            for k in range(16):
                q = q8 * 16 + k
                code = tab[o_ord + q]
                got = rrecv[p][code // 2].astype(jnp.float32)
                acc = jnp.where(code % 2 == 1, 0.0, acc) + got
                run[q] = acc
            return acc

        lax.fori_loop(0, slots // 16, add, jnp.zeros((rp, width), jnp.float32))

        @pl.loop(0, 2 * both // 16)
        def _(t8):
            for k in range(16):
                t = t8 * 16 + k
                psum[p, t] = run[tab[o_last + t]]

        remote(psum.at[p, core_part(1 - c)], rc.at[p], rcs.at[p], rcr.at[p], to_core).start()

    def rb(p):
        wait_on(rc.at[p], rcr.at[p])

        own, other = (c * 2 + place) * nif, (c * 2 + 1 - place) * nif

        @pl.loop(0, nif // 8)
        def _(i):
            here = pl.ds(own + i * 8, 8)
            psum[p, here] += rc[p, pl.ds(place * nif + i * 8, 8)]
            total = psum[p, pl.ds(other + i * 8, 8)] + rc[p, pl.ds((1 - place) * nif + i * 8, 8)]
            half[p, pl.ds(i * 8, 8)] = total.astype(jnp.bfloat16)

        remote(half.at[p], r1.at[p], r1s.at[p], r1r.at[p], to_mate).start()

    def rd(p):
        wait_on(r1.at[p], r1r.at[p])
        base = (c * 2 + place) * nif

        @pl.loop(0, nif // 4)
        def _(l4):
            ls = pl.ds(l4 * 4, 4)
            asm = psum[p, pl.ds(base + l4 * 4, 4)] + r1[p, ls].astype(jnp.float32)
            old = lam[ls, rows(p)]
            lam[ls, rows(p)] = old + (rhs[ls, rows(p)] - st[ls, rows(p)] * old - asm) * w_inv[ls, rows(p)]

        wait_on(rc.at[p], rcs.at[p])
        wait_on(r1.at[p], r1s.at[p])

    def diag1():
        load_s.wait()
        lane = lax.broadcasted_iota(jnp.int32, (rp, LANES), 1)
        row = lax.broadcasted_iota(jnp.int32, (rp, LANES), 0)
        for k in range(per_sub):
            lo = k // 2 * LANES

            @pl.loop(0, nsub)
            def _(s):
                picked = jnp.zeros((1, LANES), jnp.float32)
                for p in range(NP):
                    blk = s_buf[s, k, p, :, lo : lo + LANES].astype(jnp.float32)
                    keep = lane == row + ((k % 2) * tile + p * rp)
                    picked += jnp.sum(jnp.where(keep, blk, 0.0), axis=0, keepdims=True)
                if k % 2:
                    picked = pltpu.roll(picked, tile, 1)
                drow[s * per_sub + k] = picked

        @pl.loop(0, BLOCKS)
        def _(j):
            for k in range(cap):
                dsend[pl.ds(j * 8 + k, 1), :] = drow[tab[o_t3 + j * cap + k]]
            for k in range(cap, 8):
                dsend[pl.ds(j * 8 + k, 1), :] = jnp.zeros((1, LANES), jnp.float32)

        scatter(dsend, drecv, 8, ds.at[0], dr.at[0])

    def diag2():
        n = (BLOCKS - 1) * 8
        wait_on(drecv.at[pl.ds(0, n)], dr.at[0])
        wait_on(dsend.at[pl.ds(0, n)], ds.at[0])
        came = drecv[...].astype(jnp.bfloat16)
        want = lax.broadcasted_iota(jnp.int32, (2 * both, BLOCKS * 8), 0)
        hot = jnp.where(want == slot_tile[...], 1.0, 0.0).astype(jnp.bfloat16)
        dpart[...] = jnp.dot(hot, came, preferred_element_type=jnp.float32)
        remote(dpart.at[core_part(1 - c)], drc, ds.at[1], dr.at[1], to_core).start()

    def diag3():
        wait_on(drc, dr.at[1])
        dpart[core_part(c)] += drc[...]
        wait_on(drc, ds.at[1])
        remote(dpart.at[at(c, 1 - place)], dx, ds.at[2], dr.at[2], to_mate).start()

    def diag4():
        wait_on(dx, dr.at[2])
        dfull[...] = jnp.zeros_like(dfull)
        dfull[0:nif] = dpart[at(c, place)] + dx[...]
        wait_on(dx, ds.at[2])
        stt = stiff_t[...]
        inv = OMEGA / (stt + dfull[...].T[0:tile])
        for g in range(nif):
            w_inv[g] = jnp.broadcast_to(inv[:, g : g + 1], (tile, width))
            st[g] = jnp.broadcast_to(stt[:, g : g + 1], (tile, width))

    g0(0)
    g0(1)
    diag1()
    g1(0)
    g0(2)
    g2(0)
    g1(1)
    g2(1)
    g1(2)
    g0(3)

    @pl.loop(0, ITERS)
    def _(sweep):
        def once(stage):
            pl.when(sweep == 0)(stage)

        def ahead(*stages):
            @pl.when(sweep < ITERS - 1)
            def _():
                for stage, p in stages:
                    stage(p)

        once(diag2)
        g2(2)
        g1(3)
        once(diag3)
        a1(0)
        once(diag4)
        g2(3)
        a1(1)
        a1(2)
        a1(3)
        mm(0, sweep == ITERS - 1)
        r0(0)
        rs(0)
        mm(2, sweep == ITERS - 1)
        mm(1, sweep == ITERS - 1)
        r0(1)
        rs(1)
        r0(2)
        ra(0)
        mm(3, sweep == ITERS - 1)
        rs(2)
        rb(0)
        r0(3)
        ra(1)
        rb(1)
        rs(3)
        rd(0)
        ahead((g0, 0))
        ra(2)
        rb(2)
        rd(1)
        ahead((g0, 1), (g1, 0))
        ra(3)
        ahead((g2, 0))
        rb(3)
        rd(2)
        ahead((g1, 1), (g0, 2), (g2, 1))
        rd(3)
        ahead((g0, 3), (g1, 2))


def sweeps(plan, cid, schur, lam_start, rhs, stiff, all_owner, all_local):
    axis, kind, cap = plan
    nsub, order, _ = schur.shape
    nif, tile, width = lam_start.shape
    i32 = jnp.int32
    a, b = lax.axis_index("sub"), lax.axis_index("ifc")
    c = b % 2
    u, v, w = split(axis, a // 4, a % 4, b // 2)
    pair, _, _, across = pairing(kind, u)
    ntiles = all_owner.shape[1]
    slots = BLOCKS * cap

    def place_of(owner):
        ou, ov, ow = split(axis, owner // 32, (owner // 8) % 4, (owner // 2) % 4)
        opair, oplace, _, _ = pairing(kind, ou)
        return opair, ov * 4 + ow, (owner % 2) * 2 + oplace

    lead = join(axis, u, 0, 0)
    far = join(axis, across, 0, 0)
    size = join(axis, 1, 4, 4)

    def block(table, corner):
        cut = lax.dynamic_slice(table.reshape(4, 4, 4, 2, ntiles), (*corner, c, 0), (*size, 1, ntiles))
        return cut.reshape(16, ntiles)

    own = jnp.concatenate([block(all_owner, lead), block(all_owner, far)])
    loc = jnp.concatenate([block(all_local, lead), block(all_local, far)])
    opair, oseat, member = place_of(own)
    here = (opair == pair) & (oseat == v * 4 + w)
    before = jnp.arange(ntiles)[:, None] < jnp.arange(ntiles)[None, :]
    rank = jnp.sum((here[:, :, None] & before[None]).astype(i32), axis=1)
    tid = member * nif + loc
    match = here[:, :, None] & (rank[:, :, None] == jnp.arange(cap)[None, None, :])
    slot_tile = jnp.sum(jnp.where(match, tid[:, :, None] + 1, 0), axis=1) - 1
    flat = slot_tile.reshape(slots)
    t1 = jnp.maximum(flat, 0)
    seat = jnp.arange(slots)
    val = jnp.where(flat < 0, 4 * nif, flat)
    key = val * 256 + seat
    pos = jnp.sum((key[None, :] < key[:, None]).astype(i32), axis=1)
    first = ~jnp.any((val[None, :] == val[:, None]) & (seat[None, :] < seat[:, None]), axis=1)
    code = seat * 2 + first.astype(i32)
    order_tab = jnp.sum(jnp.where(pos[:, None] == seat[None, :], code[:, None], 0), axis=0)
    tiles = jnp.arange(4 * nif)
    upto = jnp.sum((val[None, :] <= tiles[:, None]).astype(i32), axis=1)
    has = jnp.any(val[None, :] == tiles[:, None], axis=1)
    last = jnp.where(has, upto - 1, slots)

    mine = lax.dynamic_slice_in_dim(all_owner, a * 8 + b, 1, 0)[0]
    mpair, mseat, _ = place_of(mine)
    group = jnp.where(mpair == pair, 0, 16) + mseat
    index = jnp.arange(ntiles)
    same = (group[None, :] == group[:, None]) & (index[None, :] < index[:, None])
    t2 = group * cap + jnp.sum(same.astype(i32), axis=1)
    t3 = jnp.sum(jnp.where(t2[:, None] == seat[None, :], index[:, None], 0), axis=0)
    tab = jnp.concatenate([t1, t2, t3, order_tab, last]).astype(i32)
    wide = jnp.pad(slot_tile, ((0, 0), (0, 8 - cap)), constant_values=-1).reshape(1, BLOCKS * 8)
    stiff_t = jnp.pad(stiff, ((0, LANES - nif), (0, 0)), constant_values=1.0).T

    rp = tile // NP
    per_sub = order // tile
    bf, f32 = jnp.bfloat16, jnp.float32
    vm = pltpu.VMEM
    dma = pltpu.SemaphoreType.DMA
    both = 2 * nif
    scratch = [
        vm((nsub, per_sub, NP, rp, order), bf),
        vm((ntiles, tile, width), bf),
        vm((ntiles, tile, width), bf),
        vm((nif, tile, width), f32),
        vm((nif, tile, width), f32),
        vm((slots + 1, rp, width), f32),
        vm((NP, 2 * both, rp, width), f32),
        vm((NP, slots, rp, width), bf),
        vm((NP, both, rp, width), f32),
        vm((NP, nif, rp, width), bf),
        vm((NP, nif, rp, width), bf),
        vm((ntiles, 1, LANES), f32),
        vm((BLOCKS * 8, LANES), f32),
        vm((BLOCKS * 8, LANES), f32),
        vm((2 * both, LANES), f32),
        vm((both, LANES), f32),
        vm((nif, LANES), f32),
        vm((LANES, LANES), f32),
    ]
    scratch += [vm((2 * both, rp, width), bf)] * NP
    scratch += [vm((slots, rp, width), bf)] * (2 * NP)
    scratch += [dma, dma] + [dma((NP,))] * 12 + [dma((3,))] * 2
    in_vm = pl.BlockSpec(memory_space=vm)
    lam, sens = pl.pallas_call(
        functools.partial(kernel, axis, kind, cap),
        out_shape=(
            jax.ShapeDtypeStruct((nif, tile, width), f32),
            jax.ShapeDtypeStruct((nsub, 1, width), f32),
        ),
        in_specs=[pl.BlockSpec(memory_space=pltpu.SMEM), pl.BlockSpec(memory_space=pl.ANY), in_vm, in_vm, in_vm, in_vm],
        out_specs=(in_vm, in_vm),
        scratch_shapes=scratch,
        compiler_params=pltpu.CompilerParams(
            collective_id=cid, has_side_effects=True, vmem_limit_bytes=60 * 2**20
        ),
        name="sweeps_%d_%d_%d" % plan,
    )(tab, schur.reshape(nsub, per_sub, NP, rp, order), lam_start, rhs, stiff_t, wide)
    return lam, sens.reshape(nsub, width)


def body(schur, lam_start, rhs, stiff, owner, local):
    all_owner = owner.reshape(128, 96)
    all_local = local.reshape(128, 96)
    args = (schur, lam_start, rhs, stiff, all_owner, all_local)

    def fits(plan):
        axis, kind, cap = plan
        ou, ov, ow = split(axis, all_owner // 32, (all_owner // 8) % 4, (all_owner // 2) % 4)
        group = pairing(kind, ou)[0] * 16 + ov * 4 + ow
        counts = jnp.sum((group[:, :, None] == jnp.arange(BLOCKS)).astype(jnp.int32), axis=1)
        return jnp.max(counts) <= cap

    choice = len(PLANS) - 1
    for i in reversed(range(len(PLANS) - 1)):
        choice = jnp.where(fits(PLANS[i]), i, choice)
    return lax.switch(choice, [functools.partial(sweeps, plan, i) for i, plan in enumerate(PLANS)], *args)


def solution(mesh):
    spec = P(("sub", "ifc"), None, None)
    return jax.shard_map(
        body,
        mesh=mesh,
        in_specs=(spec, spec, spec, P(("sub", "ifc"), None), P(), P()),
        out_specs=(spec, P(("sub", "ifc"), None)),
        check_vma=False,
    )
```

```python
import functools

import jax
import jax.numpy as jnp
from jax import lax
from jax.experimental import pallas as pl
from jax.experimental.pallas import tpu as pltpu
from jax.sharding import PartitionSpec as P

ITERS = 3
OMEGA = 0.7
MESH = pl.DeviceIdType.MESH
NP = 4
LANES = 128
BLOCKS = 32
PLANS = ((0, 0, 6), (1, 0, 6), (0, 0, 8))


def pairing(kind, u):
    swap, mirror = u + 1 - 2 * (u % 2), 3 - u
    if kind == 0:
        return u // 2, u % 2, swap, mirror
    return ((u + 1) // 2) % 2, u // 2, mirror, swap


def split(axis, x, y, z):
    return ((x, y, z), (y, x, z), (z, x, y))[axis]


def join(axis, u, v, w):
    return ((u, v, w), (v, u, w), (v, w, u))[axis]


def kernel(
    axis, kind, cap, tab, s_hbm, lam0, rhs, stiff_t, slot_tile,
    lam, sens,
    s_buf, z, ybf, w_inv, st, run, psum, packed, rc, r1, drow, dsend, drecv, dpart, drc, dx, dfull,
    *rest,
):
    pool, arecv, rrecv = rest[0:NP], rest[NP : 2 * NP], rest[2 * NP : 3 * NP]
    sem_s, sem_l, g0s, g0r, g1s, g1r, as_, ar, bs, br, rcs, rcr, r1s, r1r, ds, dr = rest[3 * NP :]
    nsub, per_sub, _, rp, order = s_buf.shape
    nif, tile, width = lam.shape
    slots = BLOCKS * cap
    both = 2 * nif
    ntiles = nsub * per_sub
    a, b = lax.axis_index("sub"), lax.axis_index("ifc")
    c = b % 2
    u, v, w = split(axis, a // 4, a % 4, b // 2)
    _, place, mate, across = pairing(kind, u)

    def dev(uu, vv, ww, cc):
        x, y, zz = join(axis, uu, vv, ww)
        return (x * 4 + y, zz * 2 + cc)

    to_mate, to_core = dev(mate, v, w, c), dev(u, v, w, 1 - c)
    me_v, me_w = [(v + i) % 4 for i in range(4)], [(w + i) % 4 for i in range(4)]
    seat = [v * 4 + w, 16 + v * 4 + w]
    o_t1, o_t2, o_t3 = 0, slots, slots + ntiles
    o_ord, o_last = 2 * slots + ntiles, 3 * slots + ntiles

    def remote(src, dst, ssem, rsem, to):
        return pltpu.make_async_remote_copy(
            src_ref=src, dst_ref=dst, send_sem=ssem, recv_sem=rsem, device_id=to, device_id_type=MESH
        )

    def wait_on(ref, sem):
        pltpu.make_async_copy(ref, ref, sem).wait()

    def partners(visit):
        def row(vv, first):
            for i in range(first, 4):
                for side, uu in enumerate((u, across)):
                    visit(side, side * 16 + vv * 4 + me_w[i], dev(uu, vv, me_w[i], c))

        visit(1, seat[1], dev(across, v, w, c))
        row(v, 1)

        @pl.loop(1, 4)
        def _(i):
            row((v + i) % 4, 0)

    def scatter(src, dst, n, ssem, rsem):
        def send(side, block, to):
            remote(src.at[pl.ds(block * n, n)], dst.at[pl.ds(seat[side] * n, n)], ssem, rsem, to).start()

        partners(send)
        own = pl.ds(seat[0] * n, n)
        copy = pltpu.make_async_copy(src.at[own], dst.at[own], sem_l)
        copy.start()
        copy.wait()

    load_s = pltpu.make_async_copy(s_hbm, s_buf, sem_s)
    load_s.start()

    barrier = pltpu.get_barrier_semaphore()
    for to in (to_mate, to_core):
        pl.semaphore_signal(barrier, inc=1, device_id=to, device_id_type=MESH)
    partners(lambda side, block, to: pl.semaphore_signal(barrier, inc=1, device_id=to, device_id_type=MESH))

    @pl.loop(0, nif)
    def _(l):
        lam[l] = lam0[l].astype(jnp.float32)

    run[slots] = jnp.zeros((rp, width), jnp.bfloat16)
    sens[...] = jnp.zeros_like(sens)
    pl.semaphore_wait(barrier, BLOCKS + 1)

    def at(core, which):
        return pl.ds((core * 2 + which) * nif, nif)

    def core_part(core):
        return pl.ds(core * both, both)

    def rows(p):
        return slice(p * rp, (p + 1) * rp)

    others = (BLOCKS - 1) * cap

    def g0(p):
        base = (c * 2 + place) * nif

        @pl.loop(0, nif // 8)
        def _(l):
            pool[p][pl.ds(base + l * 8, 8)] = lam[pl.ds(l * 8, 8), rows(p)].astype(jnp.bfloat16)

        own = pool[p].at[at(c, place)]
        remote(own, own, g0s.at[p], g0r.at[p], to_mate).start()

    def g1(p):
        wait_on(pool[p].at[at(c, 1 - place)], g0r.at[p])
        mine = pool[p].at[core_part(c)]
        remote(mine, mine, g1s.at[p], g1r.at[p], to_core).start()

    def g2(p):
        wait_on(pool[p].at[core_part(1 - c)], g1r.at[p])

        @pl.loop(0, slots // 16)
        def _(j):
            for k in range(16):
                q = j * 16 + k
                packed[p, q] = pool[p][tab[o_t1 + q]]

        if p > 0:
            wait_on(packed.at[p - 1, pl.ds(0, others)], as_.at[p - 1])
        scatter(packed.at[p], arecv[p], cap, as_.at[p], ar.at[p])

    def a1(p):
        wait_on(arecv[p].at[pl.ds(0, others)], ar.at[p])

        @pl.loop(0, ntiles // 16)
        def _(i):
            for k in range(16):
                t = i * 16 + k
                z[t, rows(p)] = arecv[p][tab[o_t2 + t]]

    def mm(p, last):
        flat = z.reshape(nsub, order, width)
        parts = z.reshape(nsub, per_sub, tile, width)
        outs = ybf.reshape(nsub, per_sub, tile, width)
        n = per_sub * rp

        @pl.loop(0, nsub)
        def _(s):
            lhs = s_buf[s, :, p].reshape(n, order)
            out = jnp.dot(lhs, flat[s], preferred_element_type=jnp.float32)
            outs[s, :, rows(p)] = out.astype(jnp.bfloat16).reshape(per_sub, rp, width)

            @pl.when(last)
            def _():
                prod = out * parts[s, :, rows(p)].reshape(n, width).astype(jnp.float32)
                sens[s] -= jnp.sum(prod, axis=0, keepdims=True) / order

    def r0(p):
        wait_on(pool[p].at[at(c, place)], g0s.at[p])
        wait_on(pool[p].at[core_part(c)], g1s.at[p])
        if p == NP - 1:
            wait_on(packed.at[p, pl.ds(0, others)], as_.at[p])

        @pl.loop(0, slots // 16)
        def _(j):
            for k in range(16):
                q = j * 16 + k
                packed[p, q] = ybf[tab[o_t3 + q], rows(p)]

    def rs(p):
        if p > 0:
            wait_on(packed.at[p - 1, pl.ds(0, others)], bs.at[p - 1])
        scatter(packed.at[p], rrecv[p], cap, bs.at[p], br.at[p])

    def ra(p):
        wait_on(rrecv[p].at[pl.ds(0, others)], br.at[p])
        if p == NP - 1:
            wait_on(packed.at[p, pl.ds(0, others)], bs.at[p])

        def add(q8, acc):
            for k in range(16):
                q = q8 * 16 + k
                code = tab[o_ord + q]
                got = rrecv[p][code // 2].astype(jnp.float32)
                acc = jnp.where(code % 2 == 1, 0.0, acc) + got
                run[q] = acc.astype(jnp.bfloat16)
            return acc

        lax.fori_loop(0, slots // 16, add, jnp.zeros((rp, width), jnp.float32))

        @pl.loop(0, 2 * both // 16)
        def _(t8):
            for k in range(16):
                t = t8 * 16 + k
                psum[p, t] = run[tab[o_last + t]]

        remote(psum.at[p, core_part(1 - c)], rc.at[p], rcs.at[p], rcr.at[p], to_core).start()

    def rb(p):
        wait_on(rc.at[p], rcr.at[p])

        @pl.loop(0, both // 8)
        def _(i):
            here = pl.ds(c * both + i * 8, 8)
            total = psum[p, here].astype(jnp.float32) + rc[p, pl.ds(i * 8, 8)].astype(jnp.float32)
            psum[p, here] = total.astype(jnp.bfloat16)

        remote(psum.at[p, at(c, 1 - place)], r1.at[p], r1s.at[p], r1r.at[p], to_mate).start()

    def rd(p):
        wait_on(r1.at[p], r1r.at[p])
        base = (c * 2 + place) * nif

        @pl.loop(0, nif // 4)
        def _(l4):
            ls = pl.ds(l4 * 4, 4)
            asm = psum[p, pl.ds(base + l4 * 4, 4)].astype(jnp.float32) + r1[p, ls].astype(jnp.float32)
            old = lam[ls, rows(p)]
            lam[ls, rows(p)] = old + (rhs[ls, rows(p)] - st[ls, rows(p)] * old - asm) * w_inv[ls, rows(p)]

        wait_on(rc.at[p], rcs.at[p])
        wait_on(r1.at[p], r1s.at[p])

    def diag1():
        load_s.wait()
        lane = lax.broadcasted_iota(jnp.int32, (rp, LANES), 1)
        row = lax.broadcasted_iota(jnp.int32, (rp, LANES), 0)
        for k in range(per_sub):
            lo = k // 2 * LANES

            @pl.loop(0, nsub)
            def _(s):
                picked = jnp.zeros((1, LANES), jnp.float32)
                for p in range(NP):
                    blk = s_buf[s, k, p, :, lo : lo + LANES].astype(jnp.float32)
                    keep = lane == row + ((k % 2) * tile + p * rp)
                    picked += jnp.sum(jnp.where(keep, blk, 0.0), axis=0, keepdims=True)
                if k % 2:
                    picked = pltpu.roll(picked, tile, 1)
                drow[s * per_sub + k] = picked

        @pl.loop(0, BLOCKS)
        def _(j):
            for k in range(cap):
                dsend[pl.ds(j * 8 + k, 1), :] = drow[tab[o_t3 + j * cap + k]]
            for k in range(cap, 8):
                dsend[pl.ds(j * 8 + k, 1), :] = jnp.zeros((1, LANES), jnp.float32)

        scatter(dsend, drecv, 8, ds.at[0], dr.at[0])

    def diag2():
        n = (BLOCKS - 1) * 8
        wait_on(drecv.at[pl.ds(0, n)], dr.at[0])
        wait_on(dsend.at[pl.ds(0, n)], ds.at[0])
        came = drecv[...].astype(jnp.bfloat16)
        want = lax.broadcasted_iota(jnp.int32, (2 * both, BLOCKS * 8), 0)
        hot = jnp.where(want == slot_tile[...], 1.0, 0.0).astype(jnp.bfloat16)
        dpart[...] = jnp.dot(hot, came, preferred_element_type=jnp.float32)
        remote(dpart.at[core_part(1 - c)], drc, ds.at[1], dr.at[1], to_core).start()

    def diag3():
        wait_on(drc, dr.at[1])
        dpart[core_part(c)] += drc[...]
        wait_on(drc, ds.at[1])
        remote(dpart.at[at(c, 1 - place)], dx, ds.at[2], dr.at[2], to_mate).start()

    def diag4():
        wait_on(dx, dr.at[2])
        dfull[...] = jnp.zeros_like(dfull)
        dfull[0:nif] = dpart[at(c, place)] + dx[...]
        wait_on(dx, ds.at[2])
        stt = stiff_t[...]
        inv = OMEGA / (stt + dfull[...].T[0:tile])
        for g in range(nif):
            w_inv[g] = jnp.broadcast_to(inv[:, g : g + 1], (tile, width))
            st[g] = jnp.broadcast_to(stt[:, g : g + 1], (tile, width))

    g0(0)
    g0(1)
    diag1()
    g1(0)
    g0(2)
    g2(0)
    g1(1)
    g2(1)
    g1(2)
    g0(3)

    @pl.loop(0, ITERS)
    def _(sweep):
        def once(stage):
            pl.when(sweep == 0)(stage)

        def ahead(*stages):
            @pl.when(sweep < ITERS - 1)
            def _():
                for stage, p in stages:
                    stage(p)

        g2(2)
        once(diag2)
        a1(0)
        g1(3)
        once(diag3)
        g2(3)
        a1(1)
        a1(2)
        once(diag4)
        a1(3)
        mm(0, sweep == ITERS - 1)
        r0(0)
        rs(0)
        mm(3, sweep == ITERS - 1)
        mm(2, sweep == ITERS - 1)
        mm(1, sweep == ITERS - 1)
        r0(1)
        rs(1)
        ra(0)
        r0(2)
        rs(2)
        rb(0)
        rd(0)
        ahead((g0, 0))
        ra(1)
        r0(3)
        rs(3)
        rb(1)
        ra(2)
        rb(2)
        ahead((g1, 0))
        rd(1)
        ahead((g0, 1), (g2, 0))
        ra(3)
        rd(2)
        ahead((g0, 2), (g1, 1))
        rb(3)
        ahead((g2, 1), (g1, 2))
        rd(3)
        ahead((g0, 3))


def sweeps(plan, cid, schur, lam_start, rhs, stiff, names):
    axis, kind, cap = plan
    nsub, order, _ = schur.shape
    nif, tile, width = lam_start.shape
    i32 = jnp.int32
    a, b = lax.axis_index("sub"), lax.axis_index("ifc")
    c = b % 2
    u, v, w = split(axis, a // 4, a % 4, b // 2)
    pair, _, _, across = pairing(kind, u)
    ntiles = names.shape[1]
    slots = BLOCKS * cap

    def place_of(owner):
        ou, ov, ow = split(axis, owner // 32, (owner // 8) % 4, (owner // 2) % 4)
        opair, oplace, _, _ = pairing(kind, ou)
        return opair, ov * 4 + ow, (owner % 2) * 2 + oplace

    lead = join(axis, u, 0, 0)
    far = join(axis, across, 0, 0)
    size = join(axis, 1, 4, 4)

    def block(table, corner):
        cut = lax.dynamic_slice(table.reshape(4, 4, 4, 2, ntiles), (*corner, c, 0), (*size, 1, ntiles))
        return cut.reshape(16, ntiles)

    both_sides = jnp.concatenate([block(names, lead), block(names, far)])
    own, loc = both_sides // 64, both_sides % 64
    opair, oseat, member = place_of(own)
    here = (opair == pair) & (oseat == v * 4 + w)
    before = jnp.arange(ntiles)[:, None] < jnp.arange(ntiles)[None, :]
    rank = jnp.sum((here[:, :, None] & before[None]).astype(i32), axis=1)
    tid = member * nif + loc
    match = here[:, :, None] & (rank[:, :, None] == jnp.arange(cap)[None, None, :])
    slot_tile = jnp.sum(jnp.where(match, tid[:, :, None] + 1, 0), axis=1) - 1
    flat = slot_tile.reshape(slots)
    t1 = jnp.maximum(flat, 0)
    seat = jnp.arange(slots)
    val = jnp.where(flat < 0, 4 * nif, flat)
    key = val * 256 + seat
    pos = jnp.sum((key[None, :] < key[:, None]).astype(i32), axis=1)
    first = ~jnp.any((val[None, :] == val[:, None]) & (seat[None, :] < seat[:, None]), axis=1)
    code = seat * 2 + first.astype(i32)
    order_tab = jnp.sum(jnp.where(pos[:, None] == seat[None, :], code[:, None], 0), axis=0)
    tiles = jnp.arange(4 * nif)
    upto = jnp.sum((val[None, :] <= tiles[:, None]).astype(i32), axis=1)
    has = jnp.any(val[None, :] == tiles[:, None], axis=1)
    last = jnp.where(has, upto - 1, slots)

    mine = lax.dynamic_slice_in_dim(names, a * 8 + b, 1, 0)[0] // 64
    mpair, mseat, _ = place_of(mine)
    group = jnp.where(mpair == pair, 0, 16) + mseat
    index = jnp.arange(ntiles)
    same = (group[None, :] == group[:, None]) & (index[None, :] < index[:, None])
    t2 = group * cap + jnp.sum(same.astype(i32), axis=1)
    t3 = jnp.sum(jnp.where(t2[:, None] == seat[None, :], index[:, None], 0), axis=0)
    tab = jnp.concatenate([t1, t2, t3, order_tab, last]).astype(i32)
    wide = jnp.pad(slot_tile, ((0, 0), (0, 8 - cap)), constant_values=-1).reshape(1, BLOCKS * 8)
    stiff_t = jnp.pad(stiff, ((0, LANES - nif), (0, 0)), constant_values=1.0).T

    rp = tile // NP
    per_sub = order // tile
    bf, f32 = jnp.bfloat16, jnp.float32
    vm = pltpu.VMEM
    dma = pltpu.SemaphoreType.DMA
    both = 2 * nif
    scratch = [
        vm((nsub, per_sub, NP, rp, order), bf),
        vm((ntiles, tile, width), bf),
        vm((ntiles, tile, width), bf),
        vm((nif, tile, width), f32),
        vm((nif, tile, width), f32),
        vm((slots + 1, rp, width), bf),
        vm((NP, 2 * both, rp, width), bf),
        vm((NP, slots, rp, width), bf),
        vm((NP, both, rp, width), bf),
        vm((NP, nif, rp, width), bf),
        vm((ntiles, 1, LANES), f32),
        vm((BLOCKS * 8, LANES), f32),
        vm((BLOCKS * 8, LANES), f32),
        vm((2 * both, LANES), f32),
        vm((both, LANES), f32),
        vm((nif, LANES), f32),
        vm((LANES, LANES), f32),
    ]
    scratch += [vm((2 * both, rp, width), bf)] * NP
    scratch += [vm((slots, rp, width), bf)] * (2 * NP)
    scratch += [dma, dma] + [dma((NP,))] * 12 + [dma((3,))] * 2
    in_vm = pl.BlockSpec(memory_space=vm)
    lam, sens = pl.pallas_call(
        functools.partial(kernel, axis, kind, cap),
        out_shape=(
            jax.ShapeDtypeStruct((nif, tile, width), f32),
            jax.ShapeDtypeStruct((nsub, 1, width), f32),
        ),
        in_specs=[pl.BlockSpec(memory_space=pltpu.SMEM), pl.BlockSpec(memory_space=pl.ANY), in_vm, in_vm, in_vm, in_vm],
        out_specs=(in_vm, in_vm),
        scratch_shapes=scratch,
        compiler_params=pltpu.CompilerParams(
            collective_id=cid, has_side_effects=True, vmem_limit_bytes=54 * 2**20
        ),
        name="sweeps_%d_%d_%d" % plan,
    )(tab, schur.reshape(nsub, per_sub, NP, rp, order), lam_start, rhs, stiff_t, wide)
    return lam, sens.reshape(nsub, width)


def body(schur, lam_start, rhs, stiff, owner, local):
    all_owner = owner.reshape(128, 96)
    all_local = local.reshape(128, 96)
    args = (schur, lam_start, rhs, stiff, all_owner * 64 + all_local)

    groups = []
    for axis, kind, _ in PLANS[:-1]:
        ou, ov, ow = split(axis, all_owner // 32, (all_owner // 8) % 4, (all_owner // 2) % 4)
        groups.append(pairing(kind, ou)[0] * 16 + ov * 4 + ow)
    counts = jnp.sum((jnp.stack(groups)[:, :, :, None] == jnp.arange(BLOCKS)).astype(jnp.int32), axis=2)
    most = jnp.max(counts, axis=(1, 2))
    choice = len(PLANS) - 1
    for i in reversed(range(len(PLANS) - 1)):
        choice = jnp.where(most[i] <= PLANS[i][2], i, choice)
    return lax.switch(choice, [functools.partial(sweeps, plan, i) for i, plan in enumerate(PLANS)], *args)


def solution(mesh):
    spec = P(("sub", "ifc"), None, None)
    return jax.shard_map(
        body,
        mesh=mesh,
        in_specs=(spec, spec, spec, P(("sub", "ifc"), None), P(), P()),
        out_specs=(spec, P(("sub", "ifc"), None)),
        check_vma=False,
    )
```
